512 devices in a mesh: wide: 64 (over y, z), narrow: 8 (over x, core).
Axes of the slice: x: 4, y: 8, z: 8, core: 2. Of those that a mesh axis runs over, the one named last changes fastest.
Arguments:
- amplitudes: bfloat16 [262144, 512], P('narrow', 'wide'), may hold values from -6 to 6
- integrals: bfloat16 [8, 64, 512, 1536], P('narrow', 'wide'), may hold values from -0.15625 to 0.15625
- amplitude_mask: int32 [4096, 64], P('narrow', 'wide'), may hold values 0 or 1
- integral_mask: int32 [8, 64, 8, 24], P('narrow', 'wide'), may hold values from 0 to 1
Outputs:
- residual: float32 [32768, 512], P(('narrow', 'wide'))
The draws below stay inside these ranges and needn't reach their ends.
All inputs are finite; a program needn't handle non-finite values. No bound on the sum of `amplitude_mask` on one device may be relied on, other than what follows from the above.
Results may differ from the reference program's by a relative error of at most 0.0003.
Values may be sent and summed in bfloat16 or wider, within the bound.
A program may use at most 64 MiB of HBM per device.

```python
import jax
import jax.numpy as jnp
from jax import lax

TILE = 64
CB = 512
RB = 64
OCC_DEV = 8
OP = 512
NPAIR = 262144
N_WIDE = 64
N_NARROW = 8


def draw_integral_mask(key, part):
    key = jax.random.fold_in(key, 11)
    key_level, key_block, key_tile = jax.random.split(key, 3)
    level = jax.random.randint(key_level, (N_NARROW, N_WIDE, 1, 1, 1, 1), 0, 3)
    block_draw = jax.random.randint(key_block, (N_NARROW, N_WIDE, N_NARROW, 1, 3, 1), 0, 4)
    tile_draw = jax.random.randint(key_tile, (N_NARROW, N_WIDE, N_NARROW, RB // TILE, 3, CB // TILE), 0, 4)
    keep = jnp.where(block_draw >= level, 1, 0) * jnp.where(tile_draw > 0, 1, 0)
    return keep.astype(jnp.int32).reshape(N_NARROW, N_WIDE, N_NARROW * RB // TILE, 3 * CB // TILE)


def plant(drawn, key, least, high):
    longest = drawn.shape.index(max(drawn.shape))
    spots = []
    for shift in (0, 1):
        where = [jax.random.randint(jax.random.fold_in(key, axis), (), 0, length) for axis, length in enumerate(drawn.shape)]
        where[longest] = (where[longest] + shift) % drawn.shape[longest]
        spots.append(tuple(where))
    return drawn.at[spots[0]].set(least).at[spots[1]].set(high)


def level_of(stream_key, shape, cuts, least, largest):
    def one(axis_at, blocks):
        heights = jax.random.uniform(jax.random.fold_in(jax.random.fold_in(stream_key, 6), axis_at), (blocks,), jnp.float32, least / len(cuts), largest / len(cuts))
        return jnp.repeat(jnp.exp(heights), shape[axis_at] // blocks).reshape((-1,) + (1,) * (len(shape) - axis_at - 1))

    factor_of = one(*cuts[0])
    for cut in cuts[1:]:
        factor_of = factor_of * one(*cut)
    return factor_of


def centred(rng, shape, width, bound, cuts=(), kind=jnp.bfloat16):
    factor_of = level_of(rng, shape, cuts, -0.22, 0.18) if cuts else 1.0
    values = jax.random.normal(rng, shape, jnp.float32) * width * factor_of
    return jnp.minimum(jnp.maximum(values, -bound), bound).astype(kind)


def setup_inputs(seed: int = 0) -> dict:
    seeds = jax.random.split(jax.random.key(seed), 5)
    amplitudes = centred(seeds[0], (NPAIR, OP), 1.0, 6.0, ((0, 8), (1, 64)))
    integrals = centred(seeds[1], (N_NARROW, N_WIDE, N_NARROW * RB, 3 * CB), (3 * CB) ** -0.5, 0.15625, ((0, 8), (1, 64)))
    amplitude_mask = plant((jax.random.randint(seeds[2], (NPAIR // TILE, N_WIDE), 0, 4) < 3).astype(jnp.int32), jax.random.fold_in(seeds[2], 1), 0, 1)
    integral_mask = draw_integral_mask(jax.random.fold_in(seeds[4], 71), 0)
    return dict(amplitudes=amplitudes, integrals=integrals, amplitude_mask=amplitude_mask, integral_mask=integral_mask)


def reference(amplitudes, integrals, amplitude_mask, integral_mask):
    tile_mask = jnp.repeat(jnp.repeat(amplitude_mask, TILE, axis=0), OCC_DEV, axis=1).astype(jnp.bfloat16)
    masked = amplitudes * tile_mask
    blocks = masked.reshape(N_NARROW, N_WIDE, CB, OP)
    padded = jnp.pad(blocks, ((0, 0), (1, 1), (0, 0), (0, 0)))

    def domain(owner):
        nearby = lax.dynamic_slice_in_dim(padded, owner, 3, 1).reshape(N_NARROW, 3 * CB, OP)
        values = lax.dynamic_index_in_dim(integrals, owner, 1, keepdims=False)
        flags = lax.dynamic_index_in_dim(integral_mask, owner, 1, keepdims=False)
        wide_flags = jnp.repeat(jnp.repeat(flags, TILE, axis=1), TILE, axis=2).astype(jnp.bfloat16)
        weights = values * wide_flags
        return jnp.einsum("nac,nco->ao", weights.astype(jnp.float32), nearby.astype(jnp.float32))

    per_owner = lax.map(domain, jnp.arange(N_WIDE, dtype=jnp.int32))
    per_owner = per_owner.reshape(N_WIDE, N_NARROW, RB, OP).transpose(1, 0, 2, 3)
    return per_owner.reshape(N_NARROW * N_WIDE * RB, OP)
```

```python
import jax
import jax.numpy as jnp
from jax import lax
from jax.experimental import pallas as pl
from jax.experimental.pallas import tpu as pltpu
from jax.sharding import PartitionSpec as P

MESH = pl.DeviceIdType.MESH
TILE = 64
ROW_ORDER = (0, 1, 7, 2, 6, 3, 5, 4)
NT = (((1,), (1,)), ((), ()))


def kernel(
    amp_hbm, int_hbm, amask_ref, imask_ref, out_ref,
    amp, weights, arow, masked, own, low, high, part, from_x, mine, from_core, total,
    load_sem, self_sem, a2a_send, a2a_recv, halo_send, halo_recv, x_send, x_recv, core_send, core_recv,
):
    me = lax.axis_index("wide")
    nar = lax.axis_index("narrow")
    y, z = me // 8, me % 8
    x, core = nar // 2, nar % 2
    up, down = (me + 1) % 64, (me + 63) % 64

    load_amp = pltpu.make_async_copy(amp_hbm, amp, load_sem.at[0])
    load_int = pltpu.make_async_copy(int_hbm, weights, load_sem.at[1])
    load_amp.start()
    load_int.start()

    barrier = pltpu.get_barrier_semaphore()

    def greet(i, _):
        pl.semaphore_signal(barrier, inc=1, device_id={"wide": (me + i) % 64}, device_id_type=MESH)
        return 0

    lax.fori_loop(1, 64, greet, 0)
    for k in (1, 2, 3):
        pl.semaphore_signal(barrier, inc=1, device_id={"narrow": (x + k) % 4 * 2 + core}, device_id_type=MESH)
    pl.semaphore_signal(barrier, inc=1, device_id={"narrow": x * 2 + 1 - core}, device_id_type=MESH)

    tile = lax.broadcasted_iota(jnp.int32, (64, 512), 1)
    block = lax.broadcasted_iota(jnp.int32, (64, 512), 0)
    picked = jnp.where(tile // 8 == block, amask_ref[...].astype(jnp.float32), 0.0).astype(jnp.bfloat16)
    tile = lax.broadcasted_iota(jnp.int32, (512, 512), 0)
    row = lax.broadcasted_iota(jnp.int32, (512, 512), 1)
    spread = jnp.where(tile % 8 == row // TILE, 1.0, 0.0).astype(jnp.bfloat16)
    arow[...] = jnp.dot(picked, spread, preferred_element_type=jnp.float32)

    load_amp.wait()

    def mask_block(b, _):
        keep = arow[pl.ds(b, 1), :]
        masked[b] = (amp[b].astype(jnp.float32) * keep).astype(jnp.bfloat16)
        return 0

    lax.fori_loop(0, 64, mask_block, 0, unroll=4)
    pl.semaphore_wait(barrier, 67)

    keep_self = pltpu.make_async_copy(masked.at[me], own.at[me], self_sem.at[0])
    keep_self.start()
    for r in ROW_ORDER:
        to_y = (y + 8 - r) % 8

        def send(i, _, to_y=to_y):
            to = to_y * 8 + (z + i) % 8
            pltpu.make_async_remote_copy(
                src_ref=masked.at[to], dst_ref=own.at[me], send_sem=a2a_send.at[0], recv_sem=a2a_recv.at[y],
                device_id={"wide": to}, device_id_type=MESH,
            ).start()
            return 0

        lax.fori_loop(1 if r == 0 else 0, 8, send, 0)

    col = lax.broadcasted_iota(jnp.int32, (24, 1536), 1)
    tile = lax.broadcasted_iota(jnp.int32, (24, 1536), 0)
    spread = jnp.where(col // TILE == tile, 1.0, 0.0).astype(jnp.bfloat16)
    flags = jnp.dot(imask_ref[...].astype(jnp.bfloat16), spread, preferred_element_type=jnp.float32)
    where = lax.broadcasted_iota(jnp.int32, (8, 1536), 1) // 512 + me
    flags = jnp.where((where >= 1) & (where <= 64), flags, 0.0).astype(jnp.bfloat16)
    load_int.wait()
    for m in range(8):
        rows = pl.ds(m * 64, 64)
        weights[rows, :] = weights[rows, :] * flags[m:m + 1, :]

    def column(r):
        return (y + r) % 8

    def forward(i, r):
        c = column(r)
        span = pl.ds(c * 8, 8)
        count = 7 if r == 0 else 8
        pltpu.make_async_remote_copy(
            src_ref=own.at[pl.ds(0, count)], dst_ref=own.at[pl.ds(0, count)], send_sem=a2a_send.at[0],
            recv_sem=a2a_recv.at[c], device_id={"wide": up}, device_id_type=MESH,
        ).wait_recv()
        if r == 0:
            keep_self.wait()
        for side, (dest, to) in enumerate(((low, up), (high, down))):
            pltpu.make_async_remote_copy(
                src_ref=own.at[span], dst_ref=dest.at[span], send_sem=halo_send.at[side],
                recv_sem=halo_recv.at[side, c], device_id={"wide": to}, device_id_type=MESH,
            ).start()

    def multiply(i, r):
        c = column(r)
        span = pl.ds(c * 8, 8)
        acc = lax.dot_general(
            own[span].reshape(64, 512), weights[:, 512:1024], NT, preferred_element_type=jnp.float32
        )
        for side, (buf, s) in enumerate(((low, 0), (high, 2))):
            pltpu.make_async_remote_copy(
                src_ref=buf.at[span], dst_ref=buf.at[span], send_sem=halo_send.at[side],
                recv_sem=halo_recv.at[side, c], device_id={"wide": up}, device_id_type=MESH,
            ).wait_recv()
            acc += lax.dot_general(
                buf[span].reshape(64, 512), weights[:, s * 512:(s + 1) * 512], NT,
                preferred_element_type=jnp.float32,
            )
        for k in range(4):
            part[i, k] = acc[:, k * 128:(k + 1) * 128]
        for k in (2, 1, 3):
            to = (x + k) % 4
            pltpu.make_async_remote_copy(
                src_ref=part.at[i, to], dst_ref=from_x.at[i, k - 1], send_sem=x_send.at[0],
                recv_sem=x_recv.at[i], device_id={"narrow": to * 2 + core}, device_id_type=MESH,
            ).start()

    def gather(i, r):
        pltpu.make_async_remote_copy(
            src_ref=from_x.at[i], dst_ref=from_x.at[i], send_sem=x_send.at[0],
            recv_sem=x_recv.at[i], device_id={"wide": up}, device_id_type=MESH,
        ).wait_recv()
        mine[i] = part[i, x] + from_x[i, 0] + from_x[i, 1] + from_x[i, 2]
        pltpu.make_async_remote_copy(
            src_ref=mine.at[i], dst_ref=from_core.at[i], send_sem=core_send.at[0],
            recv_sem=core_recv.at[i], device_id={"narrow": x * 2 + 1 - core}, device_id_type=MESH,
        ).start()

    def finish(i, r):
        pltpu.make_async_remote_copy(
            src_ref=mine.at[i], dst_ref=from_core.at[i], send_sem=core_send.at[0],
            recv_sem=core_recv.at[i], device_id={"wide": up}, device_id_type=MESH,
        ).wait_recv()
        total[pl.ds(column(r) * 64, 64), :] = mine[i] + from_core[i]

    lags = ((forward, 0), (multiply, 2), (gather, 4), (finish, 5))
    for step in range(8 + lags[-1][1]):
        for stage, lag in lags:
            i = step - lag
            if 0 <= i < 8:
                stage(i, ROW_ORDER[i])

    turned = total[...].T
    out_ref[...] = jnp.where(core == 0, turned[:64], turned[64:])

    def drain(ref, sem):
        pltpu.make_async_remote_copy(
            src_ref=ref, dst_ref=ref, send_sem=sem, recv_sem=core_recv.at[0],
            device_id={"wide": up}, device_id_type=MESH,
        ).wait_send()

    drain(own.at[pl.ds(0, 63)], a2a_send.at[0])
    drain(own, halo_send.at[0])
    drain(own, halo_send.at[1])
    drain(from_x, x_send.at[0])
    drain(mine, core_send.at[0])


def body(amplitudes, integrals, amplitude_mask, integral_mask):
    bf16, f32 = jnp.bfloat16, jnp.float32
    dma = pltpu.SemaphoreType.DMA
    block = (64, 8, 512)
    return pl.pallas_call(
        kernel,
        out_shape=jax.ShapeDtypeStruct((64, 512), f32),
        in_specs=[
            pl.BlockSpec(memory_space=pl.ANY),
            pl.BlockSpec(memory_space=pl.ANY),
            pl.BlockSpec(memory_space=pltpu.VMEM),
            pl.BlockSpec(memory_space=pltpu.VMEM),
        ],
        out_specs=pl.BlockSpec(memory_space=pltpu.VMEM),
        scratch_shapes=[
            pltpu.VMEM(block, bf16),
            pltpu.VMEM((512, 1536), bf16),
            pltpu.VMEM((64, 512), f32),
            pltpu.VMEM(block, bf16),
            pltpu.VMEM(block, bf16),
            pltpu.VMEM(block, bf16),
            pltpu.VMEM(block, bf16),
            pltpu.VMEM((8, 4, 64, 128), f32),
            pltpu.VMEM((8, 3, 64, 128), f32),
            pltpu.VMEM((8, 64, 128), f32),
            pltpu.VMEM((8, 64, 128), f32),
            pltpu.VMEM((512, 128), f32),
            dma((2,)),
            dma((1,)),
            dma((1,)),
            dma((8,)),
            dma((2,)),
            dma((2, 8)),
            dma((1,)),
            dma((8,)),
            dma((1,)),
            dma((8,)),
        ],
        compiler_params=pltpu.CompilerParams(
            collective_id=0, has_side_effects=True, vmem_limit_bytes=32 * 1024 * 1024
        ),
        name="ladder",
    )(
        amplitudes.reshape(64, 512, 8).transpose(0, 2, 1),
        integrals[0, 0],
        amplitude_mask.T,
        integral_mask[0, 0],
    )


def solution(mesh):
    return jax.shard_map(
        body,
        mesh=mesh,
        in_specs=(
            P("narrow", "wide"),
            P("narrow", "wide", None, None),
            P("narrow", "wide"),
            P("narrow", "wide", None, None),
        ),
        out_specs=P(("narrow", "wide"), None),
        check_vma=False,
    )
```

```python
import jax
import jax.numpy as jnp
from jax import lax
from jax.experimental import pallas as pl
from jax.experimental.pallas import tpu as pltpu
from jax.sharding import PartitionSpec as P

MESH = pl.DeviceIdType.MESH
TILE = 64
NT = (((1,), (1,)), ((), ()))
OFFSETS = (0, 1, 7, 2, 6, 3, 5, 4)
FRONT, HERE, BACK, PASS = range(4)
FRONT_DIRECT, FRONT_CHAIN, BACK_DIRECT, BACK_CHAIN, HERE_SELF, HERE_FORTH, HERE_REAR, PASS_FRONT, PASS_BACK = range(9)
LAGS = (0, 2, 4, 7, 8, 10)


def kernel(
    amp_hbm, int_hbm, amask_ref, imask_ref, out_ref,
    amp, raw, weights, arow, masked, column, near, mine, other, from_core, part, from_x, total,
    load_sem, y_send, y_recv, z_send, pass_sem, z_recv, core_send, core_recv, x_send, x_recv,
):
    me = lax.axis_index("wide")
    nar = lax.axis_index("narrow")
    y, z = me // 8, me % 8
    x, core = nar // 2, nar % 2
    turn = 1 - 2 * core
    has_front = (z + turn >= 0) & (z + turn < 8)
    has_back = (z - turn >= 0) & (z - turn < 8)
    front_w, back_w = me + turn, me - turn
    any_front = (front_w >= 0) & (front_w < 64)
    any_back = (back_w >= 0) & (back_w < 64)
    cross_front = any_front & jnp.logical_not(has_front)
    cross_back = any_back & jnp.logical_not(has_back)
    ring_front, ring_back = y * 8 + (z + 8 + turn) % 8, y * 8 + (z + 8 - turn) % 8
    past_y, prior_y = y + turn, y - turn
    pass_past = jnp.logical_not(has_back) & (past_y >= 0) & (past_y < 8)
    pass_prior = jnp.logical_not(has_front) & (prior_y >= 0) & (prior_y < 8)
    partner = {"narrow": x * 2 + 1 - core}

    def greet(device):
        pl.semaphore_signal(pltpu.get_barrier_semaphore(), inc=1, device_id=device, device_id_type=MESH)

    load_amp = pltpu.make_async_copy(amp_hbm, amp, load_sem.at[0])
    load_int = pltpu.make_async_copy(int_hbm, raw, load_sem.at[1])
    load_amp.start()
    load_int.start()
    for k in (4, 3, 5, 2, 6, 1, 7):
        greet({"wide": (y + k) % 8 * 8 + z})
        greet({"wide": y * 8 + (z + k) % 8})
    for k in (2, 1, 3):
        greet({"narrow": (x + k) % 4 * 2 + core})
    greet(partner)
    pl.when(cross_front)(lambda: greet({"wide": front_w}))
    pl.when(cross_back)(lambda: greet({"wide": back_w}))

    tile = lax.broadcasted_iota(jnp.int32, (64, 512), 1)
    block = lax.broadcasted_iota(jnp.int32, (64, 512), 0)
    picked = jnp.where(tile // 8 == block, amask_ref[...].astype(jnp.float32), 0.0).astype(jnp.bfloat16)
    tile = lax.broadcasted_iota(jnp.int32, (512, 512), 0)
    row = lax.broadcasted_iota(jnp.int32, (512, 512), 1)
    spread = jnp.where(tile % 8 == row // TILE, 1.0, 0.0).astype(jnp.bfloat16)
    arow[...] = jnp.dot(picked, spread, preferred_element_type=jnp.float32)
    load_amp.wait()

    def mask_block(b, _):
        keep = arow[pl.ds(b, 1), :]
        masked[b] = (amp[b].astype(jnp.float32) * keep).astype(jnp.bfloat16)
        return 0

    lax.fori_loop(0, 64, mask_block, 0, unroll=4)

    @pl.when(jnp.logical_not(any_front))
    def _():
        near[FRONT] = jnp.zeros((8, 8, 8, 512), jnp.bfloat16)

    @pl.when(jnp.logical_not(any_back))
    def _():
        near[BACK] = jnp.zeros((8, 8, 8, 512), jnp.bfloat16)

    pl.semaphore_wait(pltpu.get_barrier_semaphore(), 18 + cross_front.astype(jnp.int32) + cross_back.astype(jnp.int32))

    for offset in OFFSETS[1:]:
        to_y = (y + 8 - offset) % 8
        pltpu.make_async_remote_copy(
            src_ref=masked.at[pl.ds(to_y * 8, 8)], dst_ref=column.at[y], send_sem=y_send.at[0],
            recv_sem=y_recv.at[y], device_id={"wide": to_y * 8 + z}, device_id_type=MESH,
        ).start()

    def source(i):
        return (y + OFFSETS[i]) % 8

    def spread_row(i):
        c = source(i)
        if i > 0:
            pltpu.make_async_copy(column.at[0], column.at[0], y_recv.at[c]).wait()
        for rel in (0, 1, 7, 2, 6, 3, 5, 4):
            to_z = (z + 8 + turn * rel) % 8
            slab = masked.at[y * 8 + to_z] if i == 0 else column.at[c, to_z]
            if rel == 0:
                to, buf, spot, group = to_z, HERE, 0, HERE_SELF
            elif rel <= 4:
                ahead = to_z - turn
                inside = (ahead >= 0) & (ahead < 8)
                to, spot = (ahead + 8) % 8, rel - 1
                buf, group = jnp.where(inside, FRONT, PASS), jnp.where(inside, FRONT_DIRECT, PASS_FRONT)
            else:
                ahead = to_z + turn
                inside = (ahead >= 0) & (ahead < 8)
                to, spot = (ahead + 8) % 8, (rel + 1) % 8
                buf, group = jnp.where(inside, BACK, PASS), jnp.where(inside, BACK_DIRECT, PASS_BACK)
            if rel in (0, 1, 7):
                pltpu.make_async_copy(slab, near.at[buf, c, spot], z_recv.at[group, c]).start()
            else:
                pltpu.make_async_remote_copy(
                    src_ref=slab, dst_ref=near.at[buf, c, spot], send_sem=z_send.at[0],
                    recv_sem=z_recv.at[group, c], device_id={"wide": y * 8 + to}, device_id_type=MESH,
                ).start()

    def arrive(group, c, count):
        span = near.at[HERE, c, pl.ds(0, count)]
        pltpu.make_async_copy(span, span, z_recv.at[group, c]).wait()

    def hand(way, buf, c, first, count, to, to_buf, to_first, group):
        pltpu.make_async_remote_copy(
            src_ref=near.at[buf, c, pl.ds(first, count)], dst_ref=near.at[to_buf, c, pl.ds(to_first, count)],
            send_sem=pass_sem.at[way], recv_sem=z_recv.at[group, c], device_id={"wide": to}, device_id_type=MESH,
        ).start()

    def enter(i):
        c = source(i)
        arrive(jnp.where(has_front, FRONT_DIRECT, PASS_FRONT), c, 4)
        buf = jnp.where(has_front, FRONT, PASS)
        hand(0, buf, c, 0, 4, ring_front, HERE, 1, HERE_FORTH)

        @pl.when(pass_prior)
        def _():
            hand(2, PASS, c, 0, 4, prior_y * 8 + z, FRONT, 0, FRONT_DIRECT)

        arrive(jnp.where(has_back, BACK_DIRECT, PASS_BACK), c, 3)
        buf = jnp.where(has_back, BACK, PASS)
        hand(1, buf, c, 6, 2, ring_back, HERE, 5, HERE_REAR)
        hand(1, buf, c, 0, 1, ring_back, HERE, 7, HERE_REAR)

        @pl.when(pass_past)
        def _():
            hand(2, PASS, c, 6, 2, past_y * 8 + z, BACK, 6, BACK_DIRECT)
            hand(2, PASS, c, 0, 1, past_y * 8 + z, BACK, 0, BACK_DIRECT)

    def relay(i):
        c = source(i)
        arrive(HERE_SELF, c, 1)
        arrive(HERE_FORTH, c, 4)

        @pl.when(any_front)
        def _():
            hand(0, HERE, c, 0, 5, front_w, BACK, 1, BACK_CHAIN)

        arrive(HERE_REAR, c, 3)

        @pl.when(any_back)
        def _():
            hand(1, HERE, c, 5, 3, back_w, FRONT, 4, FRONT_CHAIN)
            hand(1, HERE, c, 0, 1, back_w, FRONT, 7, FRONT_CHAIN)

    def multiply(i):
        c = source(i)

        @pl.when(any_front)
        def _():
            arrive(FRONT_CHAIN, c, 4)

        @pl.when(cross_front)
        def _():
            arrive(FRONT_DIRECT, c, 4)

        @pl.when(any_back)
        def _():
            arrive(BACK_CHAIN, c, 5)

        @pl.when(cross_back)
        def _():
            arrive(BACK_DIRECT, c, 3)

        acc = None
        for buf in (HERE, FRONT, BACK):
            start = pl.multiple_of((1 + turn * (1 - buf)) * 512, 512)
            term = lax.dot_general(
                near[buf, c].reshape(64, 512), weights[:, pl.ds(start, 512)], NT, preferred_element_type=jnp.float32
            )
            acc = term if acc is None else acc + term
        mine[i] = acc[:, :256]
        other[i] = acc[:, 256:]
        pltpu.make_async_remote_copy(
            src_ref=other.at[i], dst_ref=from_core.at[i], send_sem=core_send.at[0],
            recv_sem=core_recv.at[i], device_id=partner, device_id_type=MESH,
        ).start()

    low_lanes = lax.broadcasted_iota(jnp.int32, (32, 128), 1) < 64

    def swap(i):
        pltpu.make_async_copy(from_core.at[i], from_core.at[i], core_recv.at[i]).wait()
        for pair in range(2):
            lanes = slice(pair * 128, pair * 128 + 128)
            rows = [
                mine[i, p * 8:p * 8 + 8, lanes] + from_core[i, (8 - p) % 8 * 8:(8 - p) % 8 * 8 + 8, lanes]
                for p in range(8)
            ]
            upper, lower = jnp.concatenate(rows[:4], 0), jnp.concatenate(rows[4:], 0)
            part[i, 2 * pair] = jnp.where(low_lanes, upper, pltpu.roll(lower, 64, 1))
            part[i, 2 * pair + 1] = jnp.where(low_lanes, pltpu.roll(upper, 64, 1), lower)
        for k in (2, 1, 3):
            to = (x + k) % 4
            pltpu.make_async_remote_copy(
                src_ref=part.at[i, to], dst_ref=from_x.at[i, k - 1], send_sem=x_send.at[0],
                recv_sem=x_recv.at[i], device_id={"narrow": to * 2 + core}, device_id_type=MESH,
            ).start()

    def finish(i):
        c = source(i)
        pltpu.make_async_copy(from_x.at[i], from_x.at[i], x_recv.at[i]).wait()
        done = part[i, x] + from_x[i, 0] + from_x[i, 1] + from_x[i, 2]
        turned = pltpu.roll(done, 64, 1)
        for p in range(8):
            at = (z + 8 - turn * p) % 8
            total[c * 8 + at] = (done if p < 4 else turned)[p % 4 * 8:p % 4 * 8 + 8]

    def mask_weights():
        col = lax.broadcasted_iota(jnp.int32, (24, 1536), 1)
        tile = lax.broadcasted_iota(jnp.int32, (24, 1536), 0)
        spread = jnp.where(col // TILE == tile, 1.0, 0.0).astype(jnp.bfloat16)
        flags = jnp.dot(imask_ref[...].astype(jnp.bfloat16), spread, preferred_element_type=jnp.float32)
        where = lax.broadcasted_iota(jnp.int32, (8, 1536), 1) // 512 + me
        flags = jnp.where((where >= 1) & (where <= 64), flags, 0.0).astype(jnp.bfloat16)
        load_int.wait()
        for m in range(8):
            to = pl.multiple_of(((m % 2 + core) % 2 * 4 + m // 2) * 64, 64)
            weights[pl.ds(to, 64), :] = raw[m * 64:m * 64 + 64, :] * flags[m:m + 1, :]

    stages = (spread_row, enter, relay, multiply, swap, finish)
    for step in range(8 + LAGS[-1]):
        for stage, lag in zip(stages, LAGS):
            if 0 <= step - lag < 8:
                stage(step - lag)
            if step == 0 and stage is spread_row:
                mask_weights()

    out_ref[...] = total[...].reshape(512, 128).T[:64]

    def drain(ref, sem):
        pltpu.make_async_copy(ref, ref, sem).wait()

    drain(near.at[0, pl.ds(0, 7)], y_send.at[0])
    drain(near.at[0, pl.ds(0, 5)], z_send.at[0])
    drain(near.at[0, pl.ds(0, 4)], pass_sem.at[0])
    drain(near.at[0, pl.ds(0, 3)], pass_sem.at[1])

    @pl.when(any_front)
    def _():
        drain(near.at[0, pl.ds(0, 5)], pass_sem.at[0])

    @pl.when(any_back)
    def _():
        drain(near.at[0, pl.ds(0, 4)], pass_sem.at[1])

    @pl.when(pass_prior)
    def _():
        drain(near.at[0, pl.ds(0, 4)], pass_sem.at[2])

    @pl.when(pass_past)
    def _():
        drain(near.at[0, pl.ds(0, 3)], pass_sem.at[2])

    drain(other, core_send.at[0])
    drain(from_x, x_send.at[0])


def body(amplitudes, integrals, amplitude_mask, integral_mask):
    bf16, f32 = jnp.bfloat16, jnp.float32
    dma = pltpu.SemaphoreType.DMA
    return pl.pallas_call(
        kernel,
        out_shape=jax.ShapeDtypeStruct((64, 512), f32),
        in_specs=[
            pl.BlockSpec(memory_space=pl.ANY),
            pl.BlockSpec(memory_space=pl.ANY),
            pl.BlockSpec(memory_space=pltpu.VMEM),
            pl.BlockSpec(memory_space=pltpu.VMEM),
        ],
        out_specs=pl.BlockSpec(memory_space=pltpu.VMEM),
        scratch_shapes=[
            pltpu.VMEM((64, 8, 512), bf16),
            pltpu.VMEM((512, 1536), bf16),
            pltpu.VMEM((512, 1536), bf16),
            pltpu.VMEM((64, 512), f32),
            pltpu.VMEM((64, 8, 512), bf16),
            pltpu.VMEM((8, 8, 8, 512), bf16),
            pltpu.VMEM((4, 8, 8, 8, 512), bf16),
            pltpu.VMEM((8, 64, 256), f32),
            pltpu.VMEM((8, 64, 256), f32),
            pltpu.VMEM((8, 64, 256), f32),
            pltpu.VMEM((8, 4, 32, 128), f32),
            pltpu.VMEM((8, 3, 32, 128), f32),
            pltpu.VMEM((64, 8, 128), f32),
            dma((2,)),
            dma((1,)),
            dma((8,)),
            dma((1,)),
            dma((3,)),
            dma((9, 8)),
            dma((1,)),
            dma((8,)),
            dma((1,)),
            dma((8,)),
        ],
        compiler_params=pltpu.CompilerParams(
            collective_id=0, has_side_effects=True, vmem_limit_bytes=60 * 1024 * 1024
        ),
        name="ladder",
    )(
        amplitudes.reshape(64, 512, 8).transpose(0, 2, 1),
        integrals[0, 0],
        amplitude_mask.T,
        integral_mask[0, 0],
    )


def solution(mesh):
    return jax.shard_map(
        body,
        mesh=mesh,
        in_specs=(
            P("narrow", "wide"),
            P("narrow", "wide", None, None),
            P("narrow", "wide"),
            P("narrow", "wide", None, None),
        ),
        out_specs=P(("narrow", "wide"), None),
        check_vma=False,
    )
```

```python
import jax
import jax.numpy as jnp
from jax import lax
from jax.experimental import pallas as pl
from jax.experimental.pallas import tpu as pltpu
from jax.sharding import PartitionSpec as P

MESH = pl.DeviceIdType.MESH
TILE = 64
NT = (((1,), (1,)), ((), ()))
OFFSETS = (0, 7, 1, 6, 2, 5, 3, 4)
TURNS = ((0, 1, 2, 3, 4, 5, 6, 7), (1, 0, 3, 2, 5, 4, 7, 6), (0, 2, 1, 4, 3, 6, 5, 7))
FRONT, HERE, BACK, PASS = range(4)
FRONT_DIRECT, FRONT_CHAIN, BACK_DIRECT, BACK_CHAIN, HERE_SELF, HERE_FORTH, HERE_REAR, PASS_FRONT, PASS_BACK = range(9)
LEAD = 4
LAGS = (0, 2, 5, 7, 10)


def kernel(
    amp_hbm, int_hbm, amask_ref, imask_ref, out_ref,
    amp, raw, weights, keep, masked, near, mine, other, from_core, part, from_x, total,
    amp_sem, load_sem, z_send, pass_sem, z_recv, core_send, core_recv, x_send, x_recv,
):
    me = lax.axis_index("wide")
    nar = lax.axis_index("narrow")
    y, z = me // 8, me % 8
    x, core = nar // 2, nar % 2
    turn = 1 - 2 * core
    has_front = (z + turn >= 0) & (z + turn < 8)
    has_back = (z - turn >= 0) & (z - turn < 8)
    front_w, back_w = me + turn, me - turn
    any_front = (front_w >= 0) & (front_w < 64)
    any_back = (back_w >= 0) & (back_w < 64)
    cross_front = any_front & jnp.logical_not(has_front)
    cross_back = any_back & jnp.logical_not(has_back)
    ring_front, ring_back = y * 8 + (z + 8 + turn) % 8, y * 8 + (z + 8 - turn) % 8
    past_y, prior_y = y + turn, y - turn
    pass_past = jnp.logical_not(has_back) & (past_y >= 0) & (past_y < 8)
    pass_prior = jnp.logical_not(has_front) & (prior_y >= 0) & (prior_y < 8)
    partner = {"narrow": x * 2 + 1 - core}

    def greet(device):
        pl.semaphore_signal(pltpu.get_barrier_semaphore(), inc=1, device_id=device, device_id_type=MESH)

    def greet_wide(i, _):
        greet({"wide": (me + i) % 64})
        return 0

    lax.fori_loop(32, 64, greet_wide, 0)
    lax.fori_loop(1, 32, greet_wide, 0)
    for k in (2, 1, 3):
        greet({"narrow": (x + k) % 4 * 2 + core})
    greet(partner)
    for i in range(8):
        blocks = pl.ds((y + 8 - OFFSETS[i]) % 8 * 8, 8)
        pltpu.make_async_copy(amp_hbm.at[blocks], amp.at[blocks], amp_sem.at[i]).start()
    load_int = pltpu.make_async_copy(int_hbm, raw, load_sem.at[0])
    load_int.start()

    @pl.when(jnp.logical_not(any_front))
    def _():
        near[FRONT] = jnp.zeros((8, 8, 8, 512), jnp.bfloat16)

    @pl.when(jnp.logical_not(any_back))
    def _():
        near[BACK] = jnp.zeros((8, 8, 8, 512), jnp.bfloat16)

    tile = lax.broadcasted_iota(jnp.int32, (512, 512), 1)
    row = lax.broadcasted_iota(jnp.int32, (512, 512), 0)
    picked = jnp.where(tile // 8 == row // 8, amask_ref[...].astype(jnp.float32), 0.0).astype(jnp.bfloat16)
    spread = jnp.where(row % 8 == tile // TILE, 1.0, 0.0).astype(jnp.bfloat16)
    keep[...] = jnp.dot(picked, spread, preferred_element_type=jnp.float32).astype(jnp.bfloat16).reshape(64, 8, 512)

    def mask_row(i):
        to_y = (y + 8 - OFFSETS[i]) % 8
        blocks = pl.ds(to_y * 8, 8)
        pltpu.make_async_copy(amp_hbm.at[blocks], amp.at[blocks], amp_sem.at[i]).wait()
        masked[blocks] = amp[blocks] * keep[blocks]

    mask_row(0)
    mask_row(1)
    pl.semaphore_wait(pltpu.get_barrier_semaphore(), 67)

    def source(i):
        return (y + OFFSETS[i]) % 8

    def send(i):
        to_y = (y + 8 - OFFSETS[i]) % 8
        for rel in (0, 1, 7, 2, 6, 3, 5, 4):
            to_z = (z + 8 + turn * rel) % 8
            if rel == 0:
                to, buf, spot, group = to_z, HERE, 0, HERE_SELF
            elif rel <= 4:
                ahead = to_z - turn
                inside = (ahead >= 0) & (ahead < 8)
                to, spot = (ahead + 8) % 8, rel - 1
                buf, group = jnp.where(inside, FRONT, PASS), jnp.where(inside, FRONT_DIRECT, PASS_FRONT)
            else:
                ahead = to_z + turn
                inside = (ahead >= 0) & (ahead < 8)
                to, spot = (ahead + 8) % 8, (rel + 1) % 8
                buf, group = jnp.where(inside, BACK, PASS), jnp.where(inside, BACK_DIRECT, PASS_BACK)
            slab, place, sem = masked.at[to_y * 8 + to_z], near.at[buf, y, spot], z_recv.at[group, y]
            if i == 0 and rel in (0, 1, 7):
                pltpu.make_async_copy(slab, place, sem).start()
            else:
                pltpu.make_async_remote_copy(
                    src_ref=slab, dst_ref=place, send_sem=z_send.at[0], recv_sem=sem,
                    device_id={"wide": to_y * 8 + to}, device_id_type=MESH,
                ).start()

    def arrive(group, c, count):
        span = near.at[HERE, c, pl.ds(0, count)]
        pltpu.make_async_copy(span, span, z_recv.at[group, c]).wait()

    def hand(way, buf, c, first, count, to, to_buf, to_first, group):
        pltpu.make_async_remote_copy(
            src_ref=near.at[buf, c, pl.ds(first, count)], dst_ref=near.at[to_buf, c, pl.ds(to_first, count)],
            send_sem=pass_sem.at[way], recv_sem=z_recv.at[group, c], device_id={"wide": to}, device_id_type=MESH,
        ).start()

    def enter(i):
        c = source(i)
        arrive(jnp.where(has_front, FRONT_DIRECT, PASS_FRONT), c, 4)
        buf = jnp.where(has_front, FRONT, PASS)
        hand(0, buf, c, 0, 4, ring_front, HERE, 1, HERE_FORTH)

        @pl.when(pass_prior)
        def _():
            hand(2, PASS, c, 0, 4, prior_y * 8 + z, FRONT, 0, FRONT_DIRECT)

        arrive(jnp.where(has_back, BACK_DIRECT, PASS_BACK), c, 3)
        buf = jnp.where(has_back, BACK, PASS)
        hand(1, buf, c, 6, 2, ring_back, HERE, 5, HERE_REAR)
        hand(1, buf, c, 0, 1, ring_back, HERE, 7, HERE_REAR)

        @pl.when(pass_past)
        def _():
            hand(2, PASS, c, 6, 2, past_y * 8 + z, BACK, 6, BACK_DIRECT)
            hand(2, PASS, c, 0, 1, past_y * 8 + z, BACK, 0, BACK_DIRECT)

    def relay(i):
        c = source(i)
        arrive(HERE_SELF, c, 1)
        arrive(HERE_FORTH, c, 4)

        @pl.when(any_front)
        def _():
            hand(0, HERE, c, 0, 5, front_w, BACK, 1, BACK_CHAIN)

        arrive(HERE_REAR, c, 3)

        @pl.when(any_back)
        def _():
            hand(1, HERE, c, 5, 3, back_w, FRONT, 4, FRONT_CHAIN)
            hand(1, HERE, c, 0, 1, back_w, FRONT, 7, FRONT_CHAIN)

    def turn_of(i):
        inner, first, last = (OFFSETS[order[i]] for order in TURNS)
        return (y + jnp.where(z == 0, first, jnp.where(z == 7, last, inner))) % 8

    def multiply(i):
        c = turn_of(i)

        @pl.when(any_front)
        def _():
            arrive(FRONT_CHAIN, c, 4)

        @pl.when(cross_front)
        def _():
            arrive(FRONT_DIRECT, c, 4)

        @pl.when(any_back)
        def _():
            arrive(BACK_CHAIN, c, 5)

        @pl.when(cross_back)
        def _():
            arrive(BACK_DIRECT, c, 3)

        acc = None
        for buf in (HERE, FRONT, BACK):
            start = pl.multiple_of((1 + turn * (1 - buf)) * 512, 512)
            term = lax.dot_general(
                near[buf, c].reshape(64, 512), weights[:, pl.ds(start, 512)], NT, preferred_element_type=jnp.float32
            )
            acc = term if acc is None else acc + term
        mine[i] = acc[:, :256]
        other[i] = acc[:, 256:]
        pltpu.make_async_remote_copy(
            src_ref=other.at[i], dst_ref=from_core.at[i], send_sem=core_send.at[0],
            recv_sem=core_recv.at[i], device_id=partner, device_id_type=MESH,
        ).start()

    low_lanes = lax.broadcasted_iota(jnp.int32, (32, 128), 1) < 64

    def swap(i):
        pltpu.make_async_copy(from_core.at[i], from_core.at[i], core_recv.at[i]).wait()
        for pair in range(2):
            lanes = slice(pair * 128, pair * 128 + 128)
            rows = [
                mine[i, p * 8:p * 8 + 8, lanes] + from_core[i, (8 - p) % 8 * 8:(8 - p) % 8 * 8 + 8, lanes]
                for p in range(8)
            ]
            upper, lower = jnp.concatenate(rows[:4], 0), jnp.concatenate(rows[4:], 0)
            part[i, 2 * pair] = jnp.where(low_lanes, upper, pltpu.roll(lower, 64, 1))
            part[i, 2 * pair + 1] = jnp.where(low_lanes, pltpu.roll(upper, 64, 1), lower)
        for k in (2, 1, 3):
            to = (x + k) % 4
            pltpu.make_async_remote_copy(
                src_ref=part.at[i, to], dst_ref=from_x.at[i, k - 1], send_sem=x_send.at[0],
                recv_sem=x_recv.at[i], device_id={"narrow": to * 2 + core}, device_id_type=MESH,
            ).start()

    def finish(i):
        c = turn_of(i)
        pltpu.make_async_copy(from_x.at[i], from_x.at[i], x_recv.at[i]).wait()
        done = part[i, x] + from_x[i, 0] + from_x[i, 1] + from_x[i, 2]
        turned = pltpu.roll(done, 64, 1)
        for p in range(8):
            at = (z + 8 - turn * p) % 8
            total[c * 8 + at] = (done if p < 4 else turned)[p % 4 * 8:p % 4 * 8 + 8]

    def mask_weights():
        col = lax.broadcasted_iota(jnp.int32, (24, 1536), 1)
        tile = lax.broadcasted_iota(jnp.int32, (24, 1536), 0)
        spread = jnp.where(col // TILE == tile, 1.0, 0.0).astype(jnp.bfloat16)
        flags = jnp.dot(imask_ref[...].astype(jnp.bfloat16), spread, preferred_element_type=jnp.float32)
        where = lax.broadcasted_iota(jnp.int32, (8, 1536), 1) // 512 + me
        flags = jnp.where((where >= 1) & (where <= 64), flags, 0.0).astype(jnp.bfloat16)
        load_int.wait()
        for m in range(8):
            to = pl.multiple_of(((m % 2 + core) % 2 * 4 + m // 2) * 64, 64)
            weights[pl.ds(to, 64), :] = raw[m * 64:m * 64 + 64, :] * flags[m:m + 1, :]

    for i in range(8):
        if i > 1:
            mask_row(i)
        if i < LEAD:
            send(i)
    mask_weights()
    stages = (enter, relay, multiply, swap, finish)
    for step in range(8 + LAGS[-1]):
        if step + LEAD < 8:
            send(step + LEAD)
        for stage, lag in zip(stages, LAGS):
            if 0 <= step - lag < 8:
                stage(step - lag)

    out_ref[...] = total[...].reshape(512, 128).T[:64]

    def drain(ref, sem):
        pltpu.make_async_copy(ref, ref, sem).wait()

    drain(near.at[0, pl.ds(0, 7)], z_send.at[0])
    drain(near.at[0, 7, pl.ds(0, 5)], z_send.at[0])
    drain(near.at[0, pl.ds(0, 4)], pass_sem.at[0])
    drain(near.at[0, pl.ds(0, 3)], pass_sem.at[1])

    @pl.when(any_front)
    def _():
        drain(near.at[0, pl.ds(0, 5)], pass_sem.at[0])

    @pl.when(any_back)
    def _():
        drain(near.at[0, pl.ds(0, 4)], pass_sem.at[1])

    @pl.when(pass_prior)
    def _():
        drain(near.at[0, pl.ds(0, 4)], pass_sem.at[2])

    @pl.when(pass_past)
    def _():
        drain(near.at[0, pl.ds(0, 3)], pass_sem.at[2])

    drain(other, core_send.at[0])
    drain(from_x, x_send.at[0])


def body(amplitudes, integrals, amplitude_mask, integral_mask):
    bf16, f32 = jnp.bfloat16, jnp.float32
    dma = pltpu.SemaphoreType.DMA
    return pl.pallas_call(
        kernel,
        out_shape=jax.ShapeDtypeStruct((64, 512), f32),
        in_specs=[
            pl.BlockSpec(memory_space=pl.ANY),
            pl.BlockSpec(memory_space=pl.ANY),
            pl.BlockSpec(memory_space=pltpu.VMEM),
            pl.BlockSpec(memory_space=pltpu.VMEM),
        ],
        out_specs=pl.BlockSpec(memory_space=pltpu.VMEM),
        scratch_shapes=[
            pltpu.VMEM((64, 8, 512), bf16),
            pltpu.VMEM((512, 1536), bf16),
            pltpu.VMEM((512, 1536), bf16),
            pltpu.VMEM((64, 8, 512), bf16),
            pltpu.VMEM((64, 8, 512), bf16),
            pltpu.VMEM((4, 8, 8, 8, 512), bf16),
            pltpu.VMEM((8, 64, 256), f32),
            pltpu.VMEM((8, 64, 256), f32),
            pltpu.VMEM((8, 64, 256), f32),
            pltpu.VMEM((8, 4, 32, 128), f32),
            pltpu.VMEM((8, 3, 32, 128), f32),
            pltpu.VMEM((64, 8, 128), f32),
            dma((8,)),
            dma((1,)),
            dma((1,)),
            dma((3,)),
            dma((9, 8)),
            dma((1,)),
            dma((8,)),
            dma((1,)),
            dma((8,)),
        ],
        compiler_params=pltpu.CompilerParams(
            collective_id=0, has_side_effects=True, vmem_limit_bytes=60 * 1024 * 1024
        ),
        name="ladder",
    )(
        amplitudes.reshape(64, 512, 8).transpose(0, 2, 1),
        integrals[0, 0],
        amplitude_mask.T,
        integral_mask[0, 0],
    )


def solution(mesh):
    return jax.shard_map(
        body,
        mesh=mesh,
        in_specs=(
            P("narrow", "wide"),
            P("narrow", "wide", None, None),
            P("narrow", "wide"),
            P("narrow", "wide", None, None),
        ),
        out_specs=P(("narrow", "wide"), None),
        check_vma=False,
    )
```

```python
import jax
import jax.numpy as jnp
from jax import lax
from jax.experimental import pallas as pl
from jax.experimental.pallas import tpu as pltpu
from jax.sharding import PartitionSpec as P

MESH = pl.DeviceIdType.MESH
TILE = 64
NT = (((1,), (1,)), ((), ()))
OFFSETS = (0, 7, 1, 6, 2, 5, 3, 4)
TURNS = ((0, 1, 2, 3, 4, 5, 6, 7), (1, 0, 3, 2, 5, 4, 7, 6), (0, 2, 1, 4, 3, 6, 5, 7))
FRONT, HERE, BACK, PASS = range(4)
FRONT_DIRECT, FRONT_CHAIN, BACK_DIRECT, BACK_CHAIN, HERE_SELF, HERE_FORTH, HERE_REAR, PASS_FRONT, PASS_BACK = range(9)
LEAD = 4
LAGS = (0, 2, 5, 6, 9)


def kernel(
    amp_hbm, int_hbm, amask_ref, imask_ref, out_ref,
    amp, raw, weights, keep, masked, near, mine, other, from_core, part, from_x, total,
    row_in, amp_sem, load_sem, z_send, pass_sem, z_recv, core_send, core_recv, x_send, x_recv,
):
    me = lax.axis_index("wide")
    nar = lax.axis_index("narrow")
    y, z = me // 8, me % 8
    x, core = nar // 2, nar % 2
    turn = 1 - 2 * core
    has_front = (z + turn >= 0) & (z + turn < 8)
    has_back = (z - turn >= 0) & (z - turn < 8)
    front_w, back_w = me + turn, me - turn
    any_front = (front_w >= 0) & (front_w < 64)
    any_back = (back_w >= 0) & (back_w < 64)
    cross_front = any_front & jnp.logical_not(has_front)
    cross_back = any_back & jnp.logical_not(has_back)
    ring_front, ring_back = y * 8 + (z + 8 + turn) % 8, y * 8 + (z + 8 - turn) % 8
    past_y, prior_y = y + turn, y - turn
    pass_past = jnp.logical_not(has_back) & (past_y >= 0) & (past_y < 8)
    pass_prior = jnp.logical_not(has_front) & (prior_y >= 0) & (prior_y < 8)
    partner = {"narrow": x * 2 + 1 - core}

    def greet(device):
        pl.semaphore_signal(pltpu.get_barrier_semaphore(), inc=1, device_id=device, device_id_type=MESH)

    for k in (4, 3, 5, 2, 6, 1, 7):
        greet({"wide": y * 8 + (z + k) % 8})
        greet({"wide": (y + k) % 8 * 8 + z})
    for k in (2, 1, 3):
        greet({"narrow": (x + k) % 4 * 2 + core})
    greet(partner)
    for i in range(8):
        blocks = pl.ds((y + 8 - OFFSETS[i]) % 8 * 8, 8)
        pltpu.make_async_copy(amp_hbm.at[blocks], amp.at[blocks], amp_sem.at[i]).start()
    load_int = pltpu.make_async_copy(int_hbm, raw, load_sem.at[0])
    load_int.start()

    @pl.when(jnp.logical_not(any_front))
    def _():
        near[FRONT] = jnp.zeros((8, 8, 8, 512), jnp.bfloat16)

    @pl.when(jnp.logical_not(any_back))
    def _():
        near[BACK] = jnp.zeros((8, 8, 8, 512), jnp.bfloat16)

    tile = lax.broadcasted_iota(jnp.int32, (512, 512), 1)
    row = lax.broadcasted_iota(jnp.int32, (512, 512), 0)
    picked = jnp.where(tile // 8 == row // 8, amask_ref[...].astype(jnp.float32), 0.0).astype(jnp.bfloat16)
    spread = jnp.where(row % 8 == tile // TILE, 1.0, 0.0).astype(jnp.bfloat16)
    keep[...] = jnp.dot(picked, spread, preferred_element_type=jnp.float32).astype(jnp.bfloat16).reshape(64, 8, 512)

    def mask_row(i):
        to_y = (y + 8 - OFFSETS[i]) % 8
        blocks = pl.ds(to_y * 8, 8)
        pltpu.make_async_copy(amp_hbm.at[blocks], amp.at[blocks], amp_sem.at[i]).wait()
        masked[blocks] = amp[blocks] * keep[blocks]

    mask_row(0)
    mask_row(1)
    pl.semaphore_wait(pltpu.get_barrier_semaphore(), 18)
    for k in (4, 3, 5, 2, 6, 1, 7):
        pl.semaphore_signal(row_in.at[y], inc=1, device_id={"wide": (y + k) % 8 * 8 + z}, device_id_type=MESH)

    def source(i):
        return (y + OFFSETS[i]) % 8

    def send(i):
        to_y = (y + 8 - OFFSETS[i]) % 8
        if i > 0:
            pl.semaphore_wait(row_in.at[to_y], 1)
        for rel in (0, 1, 7, 2, 6, 3, 5, 4):
            to_z = (z + 8 + turn * rel) % 8
            if rel == 0:
                to, buf, spot, group = to_z, HERE, 0, HERE_SELF
            elif rel <= 4:
                ahead = to_z - turn
                inside = (ahead >= 0) & (ahead < 8)
                to, spot = (ahead + 8) % 8, rel - 1
                buf, group = jnp.where(inside, FRONT, PASS), jnp.where(inside, FRONT_DIRECT, PASS_FRONT)
            else:
                ahead = to_z + turn
                inside = (ahead >= 0) & (ahead < 8)
                to, spot = (ahead + 8) % 8, (rel + 1) % 8
                buf, group = jnp.where(inside, BACK, PASS), jnp.where(inside, BACK_DIRECT, PASS_BACK)
            slab, place, sem = masked.at[to_y * 8 + to_z], near.at[buf, y, spot], z_recv.at[group, y]
            if i == 0 and rel in (0, 1, 7):
                pltpu.make_async_copy(slab, place, sem).start()
            else:
                pltpu.make_async_remote_copy(
                    src_ref=slab, dst_ref=place, send_sem=z_send.at[0], recv_sem=sem,
                    device_id={"wide": to_y * 8 + to}, device_id_type=MESH,
                ).start()

    def arrive(group, c, count):
        span = near.at[HERE, c, pl.ds(0, count)]
        pltpu.make_async_copy(span, span, z_recv.at[group, c]).wait()

    def hand(way, buf, c, first, count, to, to_buf, to_first, group):
        pltpu.make_async_remote_copy(
            src_ref=near.at[buf, c, pl.ds(first, count)], dst_ref=near.at[to_buf, c, pl.ds(to_first, count)],
            send_sem=pass_sem.at[way], recv_sem=z_recv.at[group, c], device_id={"wide": to}, device_id_type=MESH,
        ).start()

    def enter(i):
        c = source(i)
        arrive(jnp.where(has_front, FRONT_DIRECT, PASS_FRONT), c, 4)
        buf = jnp.where(has_front, FRONT, PASS)
        hand(0, buf, c, 0, 4, ring_front, HERE, 1, HERE_FORTH)

        @pl.when(pass_prior)
        def _():
            hand(2, PASS, c, 0, 4, prior_y * 8 + z, FRONT, 0, FRONT_DIRECT)

        arrive(jnp.where(has_back, BACK_DIRECT, PASS_BACK), c, 3)
        buf = jnp.where(has_back, BACK, PASS)
        hand(1, buf, c, 6, 2, ring_back, HERE, 5, HERE_REAR)
        hand(1, buf, c, 0, 1, ring_back, HERE, 7, HERE_REAR)

        @pl.when(pass_past)
        def _():
            hand(2, PASS, c, 6, 2, past_y * 8 + z, BACK, 6, BACK_DIRECT)
            hand(2, PASS, c, 0, 1, past_y * 8 + z, BACK, 0, BACK_DIRECT)

    def relay(i):
        c = source(i)
        arrive(HERE_SELF, c, 1)
        arrive(HERE_FORTH, c, 4)

        @pl.when(any_front)
        def _():
            hand(0, HERE, c, 0, 5, front_w, BACK, 1, BACK_CHAIN)

        arrive(HERE_REAR, c, 3)

        @pl.when(any_back)
        def _():
            hand(1, HERE, c, 5, 3, back_w, FRONT, 4, FRONT_CHAIN)
            hand(1, HERE, c, 0, 1, back_w, FRONT, 7, FRONT_CHAIN)

    def turn_of(i):
        inner, first, last = (OFFSETS[order[i]] for order in TURNS)
        return (y + jnp.where(z == 0, first, jnp.where(z == 7, last, inner))) % 8

    def multiply(i):
        c = turn_of(i)

        @pl.when(any_front)
        def _():
            arrive(FRONT_CHAIN, c, 4)

        @pl.when(cross_front)
        def _():
            arrive(FRONT_DIRECT, c, 4)

        @pl.when(any_back)
        def _():
            arrive(BACK_CHAIN, c, 5)

        @pl.when(cross_back)
        def _():
            arrive(BACK_DIRECT, c, 3)

        acc = None
        for buf in (HERE, FRONT, BACK):
            start = pl.multiple_of((1 + turn * (1 - buf)) * 512, 512)
            term = lax.dot_general(
                near[buf, c].reshape(64, 512), weights[:, pl.ds(start, 512)], NT, preferred_element_type=jnp.float32
            )
            acc = term if acc is None else acc + term
        mine[i] = acc[:, :256]
        other[i] = acc[:, 256:]
        pltpu.make_async_remote_copy(
            src_ref=other.at[i], dst_ref=from_core.at[i], send_sem=core_send.at[0],
            recv_sem=core_recv.at[i], device_id=partner, device_id_type=MESH,
        ).start()

    low_lanes = lax.broadcasted_iota(jnp.int32, (32, 128), 1) < 64

    def swap(i):
        pltpu.make_async_copy(from_core.at[i], from_core.at[i], core_recv.at[i]).wait()
        for pair in range(2):
            lanes = slice(pair * 128, pair * 128 + 128)
            rows = [
                mine[i, p * 8:p * 8 + 8, lanes] + from_core[i, (8 - p) % 8 * 8:(8 - p) % 8 * 8 + 8, lanes]
                for p in range(8)
            ]
            upper, lower = jnp.concatenate(rows[:4], 0), jnp.concatenate(rows[4:], 0)
            part[i, 2 * pair] = jnp.where(low_lanes, upper, pltpu.roll(lower, 64, 1))
            part[i, 2 * pair + 1] = jnp.where(low_lanes, pltpu.roll(upper, 64, 1), lower)
        for k in (2, 1, 3):
            to = (x + k) % 4
            pltpu.make_async_remote_copy(
                src_ref=part.at[i, to], dst_ref=from_x.at[i, k - 1], send_sem=x_send.at[0],
                recv_sem=x_recv.at[i], device_id={"narrow": to * 2 + core}, device_id_type=MESH,
            ).start()

    def finish(i):
        c = turn_of(i)
        pltpu.make_async_copy(from_x.at[i], from_x.at[i], x_recv.at[i]).wait()
        done = part[i, x] + from_x[i, 0] + from_x[i, 1] + from_x[i, 2]
        turned = pltpu.roll(done, 64, 1)
        for p in range(8):
            at = (z + 8 - turn * p) % 8
            total[c * 8 + at] = (done if p < 4 else turned)[p % 4 * 8:p % 4 * 8 + 8]

    def mask_weights():
        col = lax.broadcasted_iota(jnp.int32, (24, 1536), 1)
        tile = lax.broadcasted_iota(jnp.int32, (24, 1536), 0)
        spread = jnp.where(col // TILE == tile, 1.0, 0.0).astype(jnp.bfloat16)
        flags = jnp.dot(imask_ref[...].astype(jnp.bfloat16), spread, preferred_element_type=jnp.float32)
        where = lax.broadcasted_iota(jnp.int32, (8, 1536), 1) // 512 + me
        flags = jnp.where((where >= 1) & (where <= 64), flags, 0.0).astype(jnp.bfloat16)
        load_int.wait()
        for m in range(8):
            to = pl.multiple_of(((m % 2 + core) % 2 * 4 + m // 2) * 64, 64)
            weights[pl.ds(to, 64), :] = raw[m * 64:m * 64 + 64, :] * flags[m:m + 1, :]

    send(0)
    for i in range(2, 8):
        mask_row(i)
    for i in range(1, LEAD):
        send(i)
    mask_weights()
    stages = (enter, relay, multiply, swap, finish)
    for step in range(8 + LAGS[-1]):
        if step + LEAD < 8:
            send(step + LEAD)
        for stage, lag in zip(stages, LAGS):
            if 0 <= step - lag < 8:
                stage(step - lag)

    out_ref[...] = total[...].reshape(512, 128).T[:64]

    def drain(ref, sem):
        pltpu.make_async_copy(ref, ref, sem).wait()

    drain(near.at[0, pl.ds(0, 7)], z_send.at[0])
    drain(near.at[0, 7, pl.ds(0, 5)], z_send.at[0])
    drain(near.at[0, pl.ds(0, 4)], pass_sem.at[0])
    drain(near.at[0, pl.ds(0, 3)], pass_sem.at[1])

    @pl.when(any_front)
    def _():
        drain(near.at[0, pl.ds(0, 5)], pass_sem.at[0])

    @pl.when(any_back)
    def _():
        drain(near.at[0, pl.ds(0, 4)], pass_sem.at[1])

    @pl.when(pass_prior)
    def _():
        drain(near.at[0, pl.ds(0, 4)], pass_sem.at[2])

    @pl.when(pass_past)
    def _():
        drain(near.at[0, pl.ds(0, 3)], pass_sem.at[2])

    drain(other, core_send.at[0])
    drain(from_x, x_send.at[0])


def body(amplitudes, integrals, amplitude_mask, integral_mask):
    bf16, f32 = jnp.bfloat16, jnp.float32
    dma = pltpu.SemaphoreType.DMA
    return pl.pallas_call(
        kernel,
        out_shape=jax.ShapeDtypeStruct((64, 512), f32),
        in_specs=[
            pl.BlockSpec(memory_space=pl.ANY),
            pl.BlockSpec(memory_space=pl.ANY),
            pl.BlockSpec(memory_space=pltpu.VMEM),
            pl.BlockSpec(memory_space=pltpu.VMEM),
        ],
        out_specs=pl.BlockSpec(memory_space=pltpu.VMEM),
        scratch_shapes=[
            pltpu.VMEM((64, 8, 512), bf16),
            pltpu.VMEM((512, 1536), bf16),
            pltpu.VMEM((512, 1536), bf16),
            pltpu.VMEM((64, 8, 512), bf16),
            pltpu.VMEM((64, 8, 512), bf16),
            pltpu.VMEM((4, 8, 8, 8, 512), bf16),
            pltpu.VMEM((8, 64, 256), f32),
            pltpu.VMEM((8, 64, 256), f32),
            pltpu.VMEM((8, 64, 256), f32),
            pltpu.VMEM((8, 4, 32, 128), f32),
            pltpu.VMEM((8, 3, 32, 128), f32),
            pltpu.VMEM((64, 8, 128), f32),
            pltpu.SemaphoreType.REGULAR((8,)),
            dma((8,)),
            dma((1,)),
            dma((1,)),
            dma((3,)),
            dma((9, 8)),
            dma((1,)),
            dma((8,)),
            dma((1,)),
            dma((8,)),
        ],
        compiler_params=pltpu.CompilerParams(
            collective_id=0, has_side_effects=True, vmem_limit_bytes=60 * 1024 * 1024
        ),
        name="ladder",
    )(
        amplitudes.reshape(64, 512, 8).transpose(0, 2, 1),
        integrals[0, 0],
        amplitude_mask.T,
        integral_mask[0, 0],
    )


def solution(mesh):
    return jax.shard_map(
        body,
        mesh=mesh,
        in_specs=(
            P("narrow", "wide"),
            P("narrow", "wide", None, None),
            P("narrow", "wide"),
            P("narrow", "wide", None, None),
        ),
        out_specs=P(("narrow", "wide"), None),
        check_vma=False,
    )
```

```python
import jax
import jax.numpy as jnp
from jax import lax
from jax.experimental import pallas as pl
from jax.experimental.pallas import tpu as pltpu
from jax.sharding import PartitionSpec as P

MESH = pl.DeviceIdType.MESH
TILE = 64
OFFSETS = (0, 7, 1, 6, 2, 5, 3, 4)
TURNS = ((0, 1, 2, 3, 4, 5, 6, 7), (1, 0, 3, 2, 5, 4, 7, 6), (0, 2, 1, 4, 3, 6, 5, 7))
FRONT, HERE, BACK, PASS = range(4)
FRONT_DIRECT, FRONT_CHAIN, BACK_DIRECT, BACK_CHAIN, HERE_SELF, HERE_FORTH, HERE_REAR, PASS_FRONT, PASS_BACK = range(9)
LEAD = 4
LAGS = (0, 2, 5, 6, 10)


def kernel(
    amp_hbm, int_hbm, amask_hbm, imask_hbm, out_hbm,
    out, amask, imask, flag_rows, amp, raw, weights, keep, masked, near, mine, other, from_core, part, from_x, total,
    row_in, mask_sem, amp_sem, load_sem, z_send, pass_sem, z_recv, core_send, core_recv, x_send, x_recv,
):
    me = lax.axis_index("wide")
    nar = lax.axis_index("narrow")
    y, z = me // 8, me % 8
    x, core = nar // 2, nar % 2
    turn = 1 - 2 * core
    has_front = (z + turn >= 0) & (z + turn < 8)
    has_back = (z - turn >= 0) & (z - turn < 8)
    front_w, back_w = me + turn, me - turn
    any_front = (front_w >= 0) & (front_w < 64)
    any_back = (back_w >= 0) & (back_w < 64)
    cross_front = any_front & jnp.logical_not(has_front)
    cross_back = any_back & jnp.logical_not(has_back)
    ring_front, ring_back = y * 8 + (z + 8 + turn) % 8, y * 8 + (z + 8 - turn) % 8
    past_y, prior_y = y + turn, y - turn
    pass_past = jnp.logical_not(has_back) & (past_y >= 0) & (past_y < 8)
    pass_prior = jnp.logical_not(has_front) & (prior_y >= 0) & (prior_y < 8)
    partner = {"narrow": x * 2 + 1 - core}

    def greet(device):
        pl.semaphore_signal(pltpu.get_barrier_semaphore(), inc=1, device_id=device, device_id_type=MESH)

    for k in (4, 3, 5, 2, 6, 1, 7):
        greet({"wide": y * 8 + (z + k) % 8})
        greet({"wide": (y + k) % 8 * 8 + z})
    for k in (2, 1, 3):
        greet({"narrow": (x + k) % 4 * 2 + core})
    greet(partner)
    load_amask = pltpu.make_async_copy(amask_hbm, amask, mask_sem.at[0])
    load_imask = pltpu.make_async_copy(imask_hbm, imask, mask_sem.at[1])
    load_amask.start()
    for i in range(8):
        blocks = pl.ds((y + 8 - OFFSETS[i]) % 8 * 8, 8)
        pltpu.make_async_copy(amp_hbm.at[blocks], amp.at[blocks], amp_sem.at[i]).start()
    load_int = pltpu.make_async_copy(int_hbm, raw, load_sem.at[0])
    load_int.start()
    load_imask.start()

    @pl.when(jnp.logical_not(any_front))
    def _():
        near[FRONT] = jnp.zeros((8, 8, 8, 512), jnp.bfloat16)

    @pl.when(jnp.logical_not(any_back))
    def _():
        near[BACK] = jnp.zeros((8, 8, 8, 512), jnp.bfloat16)

    tile = lax.broadcasted_iota(jnp.int32, (512, 512), 1)
    row = lax.broadcasted_iota(jnp.int32, (512, 512), 0)
    load_amask.wait()
    picked = jnp.where(tile // 8 == row // 8, amask[...].astype(jnp.float32), 0.0).astype(jnp.bfloat16)
    spread = jnp.where(row % 8 == tile // TILE, 1.0, 0.0).astype(jnp.bfloat16)
    keep[...] = jnp.dot(picked, spread, preferred_element_type=jnp.float32).astype(jnp.bfloat16).reshape(64, 8, 512)

    def mask_row(i):
        to_y = (y + 8 - OFFSETS[i]) % 8
        blocks = pl.ds(to_y * 8, 8)
        pltpu.make_async_copy(amp_hbm.at[blocks], amp.at[blocks], amp_sem.at[i]).wait()
        masked[blocks] = amp[blocks] * keep[blocks]

    mask_row(0)
    mask_row(1)
    pl.semaphore_wait(pltpu.get_barrier_semaphore(), 18)
    for k in (4, 3, 5, 2, 6, 1, 7):
        pl.semaphore_signal(row_in.at[y], inc=1, device_id={"wide": (y + k) % 8 * 8 + z}, device_id_type=MESH)

    def source(i):
        return (y + OFFSETS[i]) % 8

    def send(i):
        to_y = (y + 8 - OFFSETS[i]) % 8
        if i > 0:
            pl.semaphore_wait(row_in.at[to_y], 1)
        for rel in (0, 1, 7, 2, 6, 3, 5, 4):
            to_z = (z + 8 + turn * rel) % 8
            if rel == 0:
                to, buf, spot, group = to_z, HERE, 0, HERE_SELF
            elif rel <= 4:
                ahead = to_z - turn
                inside = (ahead >= 0) & (ahead < 8)
                to, spot = (ahead + 8) % 8, rel - 1
                buf, group = jnp.where(inside, FRONT, PASS), jnp.where(inside, FRONT_DIRECT, PASS_FRONT)
            else:
                ahead = to_z + turn
                inside = (ahead >= 0) & (ahead < 8)
                to, spot = (ahead + 8) % 8, (rel + 1) % 8
                buf, group = jnp.where(inside, BACK, PASS), jnp.where(inside, BACK_DIRECT, PASS_BACK)
            slab, place, sem = masked.at[to_y * 8 + to_z], near.at[buf, y, spot], z_recv.at[group, y]
            if i == 0 and rel in (0, 1, 7):
                pltpu.make_async_copy(slab, place, sem).start()
            else:
                pltpu.make_async_remote_copy(
                    src_ref=slab, dst_ref=place, send_sem=z_send.at[0], recv_sem=sem,
                    device_id={"wide": to_y * 8 + to}, device_id_type=MESH,
                ).start()

    def arrive(group, c, count):
        span = near.at[HERE, c, pl.ds(0, count)]
        pltpu.make_async_copy(span, span, z_recv.at[group, c]).wait()

    def hand(way, buf, c, first, count, to, to_buf, to_first, group):
        pltpu.make_async_remote_copy(
            src_ref=near.at[buf, c, pl.ds(first, count)], dst_ref=near.at[to_buf, c, pl.ds(to_first, count)],
            send_sem=pass_sem.at[way], recv_sem=z_recv.at[group, c], device_id={"wide": to}, device_id_type=MESH,
        ).start()

    def enter(i):
        c = source(i)
        arrive(jnp.where(has_front, FRONT_DIRECT, PASS_FRONT), c, 4)
        buf = jnp.where(has_front, FRONT, PASS)
        hand(0, buf, c, 0, 4, ring_front, HERE, 1, HERE_FORTH)

        @pl.when(pass_prior)
        def _():
            hand(2, PASS, c, 0, 4, prior_y * 8 + z, FRONT, 0, FRONT_DIRECT)

        arrive(jnp.where(has_back, BACK_DIRECT, PASS_BACK), c, 3)
        buf = jnp.where(has_back, BACK, PASS)
        hand(1, buf, c, 6, 2, ring_back, HERE, 5, HERE_REAR)
        hand(1, buf, c, 0, 1, ring_back, HERE, 7, HERE_REAR)

        @pl.when(pass_past)
        def _():
            hand(2, PASS, c, 6, 2, past_y * 8 + z, BACK, 6, BACK_DIRECT)
            hand(2, PASS, c, 0, 1, past_y * 8 + z, BACK, 0, BACK_DIRECT)

    def relay(i):
        c = source(i)
        arrive(HERE_SELF, c, 1)
        arrive(HERE_FORTH, c, 4)

        @pl.when(any_front)
        def _():
            hand(0, HERE, c, 0, 5, front_w, BACK, 1, BACK_CHAIN)

        arrive(HERE_REAR, c, 3)

        @pl.when(any_back)
        def _():
            hand(1, HERE, c, 5, 3, back_w, FRONT, 4, FRONT_CHAIN)
            hand(1, HERE, c, 0, 1, back_w, FRONT, 7, FRONT_CHAIN)

    def turn_of(i):
        inner, first, last = (OFFSETS[order[i]] for order in TURNS)
        return (y + jnp.where(z == 0, first, jnp.where(z == 7, last, inner))) % 8

    def multiply(i):
        c = turn_of(i)

        @pl.when(any_front)
        def _():
            arrive(FRONT_CHAIN, c, 4)

        @pl.when(cross_front)
        def _():
            arrive(FRONT_DIRECT, c, 4)

        @pl.when(any_back)
        def _():
            arrive(BACK_CHAIN, c, 5)

        @pl.when(cross_back)
        def _():
            arrive(BACK_DIRECT, c, 3)

        acc = None
        for buf in (HERE, FRONT, BACK):
            start = pl.multiple_of((1 + turn * (1 - buf)) * 512, 512)
            term = jnp.dot(
                near[buf, c].reshape(64, 512), weights[pl.ds(start, 512), :], preferred_element_type=jnp.float32
            )
            acc = term if acc is None else acc + term
        mine[i] = acc[:, :256]
        other[i] = acc[:, 256:]
        pltpu.make_async_remote_copy(
            src_ref=other.at[i], dst_ref=from_core.at[i], send_sem=core_send.at[0],
            recv_sem=core_recv.at[i], device_id=partner, device_id_type=MESH,
        ).start()

    low_lanes = lax.broadcasted_iota(jnp.int32, (32, 128), 1) < 64

    def swap(i):
        pltpu.make_async_copy(from_core.at[i], from_core.at[i], core_recv.at[i]).wait()
        for pair in range(2):
            lanes = slice(pair * 128, pair * 128 + 128)
            rows = [
                mine[i, p * 8:p * 8 + 8, lanes] + from_core[i, (8 - p) % 8 * 8:(8 - p) % 8 * 8 + 8, lanes]
                for p in range(8)
            ]
            upper, lower = jnp.concatenate(rows[:4], 0), jnp.concatenate(rows[4:], 0)
            part[i, 2 * pair] = jnp.where(low_lanes, upper, pltpu.roll(lower, 64, 1))
            part[i, 2 * pair + 1] = jnp.where(low_lanes, pltpu.roll(upper, 64, 1), lower)
        for k in (2, 1, 3):
            to = (x + k) % 4
            pltpu.make_async_remote_copy(
                src_ref=part.at[i, to], dst_ref=from_x.at[i, k - 1], send_sem=x_send.at[0],
                recv_sem=x_recv.at[i], device_id={"narrow": to * 2 + core}, device_id_type=MESH,
            ).start()

    def finish(i):
        c = turn_of(i)
        pltpu.make_async_copy(from_x.at[i], from_x.at[i], x_recv.at[i]).wait()
        done = part[i, x] + from_x[i, 0] + from_x[i, 1] + from_x[i, 2]
        turned = pltpu.roll(done, 64, 1)
        for p in range(8):
            at = (z + 8 - turn * p) % 8
            total[c * 8 + at] = (done if p < 4 else turned)[p % 4 * 8:p % 4 * 8 + 8]

    def mask_weights():
        col = lax.broadcasted_iota(jnp.int32, (24, 1536), 1)
        tile = lax.broadcasted_iota(jnp.int32, (24, 1536), 0)
        spread = jnp.where(col // TILE == tile, 1.0, 0.0).astype(jnp.bfloat16)
        load_imask.wait()
        flags = jnp.dot(imask[...].astype(jnp.bfloat16), spread, preferred_element_type=jnp.float32)
        where = lax.broadcasted_iota(jnp.int32, (8, 1536), 1) // 512 + me
        flags = jnp.where((where >= 1) & (where <= 64), flags, 0.0)
        load_int.wait()
        flag_rows[...] = flags
        for half in range(2):
            for pair in range(2):
                parts = []
                for k in range(2):
                    m = 2 * (2 * pair + k) + (core + half) % 2
                    rows = raw[pl.ds(pl.multiple_of(m * 64, 64), 64), :]
                    parts.append(rows * flag_rows[pl.ds(m, 1), :].astype(jnp.bfloat16))
                lanes = slice(half * 256 + pair * 128, half * 256 + pair * 128 + 128)
                weights[:, lanes] = jnp.concatenate(parts, 0).T

    send(0)
    for i in range(2, 8):
        mask_row(i)
    for i in range(1, LEAD):
        send(i)
    stages = (enter, relay, multiply, swap, finish)
    for step in range(8 + LAGS[-1]):
        if step + LEAD < 8:
            send(step + LEAD)
        if step == 2:
            mask_weights()
        for stage, lag in zip(stages, LAGS):
            if 0 <= step - lag < 8:
                stage(step - lag)

    out[...] = total[...].reshape(512, 128).T[:64]
    store = pltpu.make_async_copy(out, out_hbm, mask_sem.at[0])
    store.start()

    def drain(ref, sem):
        pltpu.make_async_copy(ref, ref, sem).wait()

    drain(near.at[0, pl.ds(0, 7)], z_send.at[0])
    drain(near.at[0, 7, pl.ds(0, 5)], z_send.at[0])
    drain(near.at[0, pl.ds(0, 4)], pass_sem.at[0])
    drain(near.at[0, pl.ds(0, 3)], pass_sem.at[1])

    @pl.when(any_front)
    def _():
        drain(near.at[0, pl.ds(0, 5)], pass_sem.at[0])

    @pl.when(any_back)
    def _():
        drain(near.at[0, pl.ds(0, 4)], pass_sem.at[1])

    @pl.when(pass_prior)
    def _():
        drain(near.at[0, pl.ds(0, 4)], pass_sem.at[2])

    @pl.when(pass_past)
    def _():
        drain(near.at[0, pl.ds(0, 3)], pass_sem.at[2])

    drain(other, core_send.at[0])
    drain(from_x, x_send.at[0])
    store.wait()


def body(amplitudes, integrals, amplitude_mask, integral_mask):
    bf16, f32 = jnp.bfloat16, jnp.float32
    dma = pltpu.SemaphoreType.DMA
    return pl.pallas_call(
        kernel,
        out_shape=jax.ShapeDtypeStruct((64, 512), f32),
        in_specs=[
            pl.BlockSpec(memory_space=pl.ANY),
            pl.BlockSpec(memory_space=pl.ANY),
            pl.BlockSpec(memory_space=pl.ANY),
            pl.BlockSpec(memory_space=pl.ANY),
        ],
        out_specs=pl.BlockSpec(memory_space=pl.ANY),
        scratch_shapes=[
            pltpu.VMEM((64, 512), f32),
            pltpu.VMEM((1, 512), jnp.int32),
            pltpu.VMEM((8, 24), jnp.int32),
            pltpu.VMEM((8, 1536), f32),
            pltpu.VMEM((64, 8, 512), bf16),
            pltpu.VMEM((512, 1536), bf16),
            pltpu.VMEM((1536, 512), bf16),
            pltpu.VMEM((64, 8, 512), bf16),
            pltpu.VMEM((64, 8, 512), bf16),
            pltpu.VMEM((4, 8, 8, 8, 512), bf16),
            pltpu.VMEM((8, 64, 256), f32),
            pltpu.VMEM((8, 64, 256), f32),
            pltpu.VMEM((8, 64, 256), f32),
            pltpu.VMEM((8, 4, 32, 128), f32),
            pltpu.VMEM((8, 3, 32, 128), f32),
            pltpu.VMEM((64, 8, 128), f32),
            pltpu.SemaphoreType.REGULAR((8,)),
            dma((2,)),
            dma((8,)),
            dma((1,)),
            dma((1,)),
            dma((3,)),
            dma((9, 8)),
            dma((1,)),
            dma((8,)),
            dma((1,)),
            dma((8,)),
        ],
        compiler_params=pltpu.CompilerParams(
            collective_id=0, has_side_effects=True, vmem_limit_bytes=60 * 1024 * 1024
        ),
        name="ladder",
    )(
        amplitudes.reshape(64, 512, 8).transpose(0, 2, 1),
        integrals[0, 0],
        amplitude_mask.T,
        integral_mask[0, 0],
    )


def solution(mesh):
    return jax.shard_map(
        body,
        mesh=mesh,
        in_specs=(
            P("narrow", "wide"),
            P("narrow", "wide", None, None),
            P("narrow", "wide"),
            P("narrow", "wide", None, None),
        ),
        out_specs=P(("narrow", "wide"), None),
        check_vma=False,
    )
```

```python
import jax
import jax.numpy as jnp
from jax import lax
from jax.experimental import pallas as pl
from jax.experimental.pallas import tpu as pltpu
from jax.sharding import PartitionSpec as P

MESH = pl.DeviceIdType.MESH
TILE = 64
OFFSETS = (0, 7, 1, 6, 2, 5, 3, 4)
TURNS = ((0, 1, 2, 3, 4, 5, 6, 7), (1, 0, 3, 2, 5, 4, 7, 6), (0, 2, 1, 4, 3, 6, 5, 7))
FRONT, HERE, BACK, PASS = range(4)
FRONT_DIRECT, FRONT_CHAIN, BACK_DIRECT, BACK_CHAIN, HERE_SELF, HERE_FORTH, HERE_REAR, PASS_FRONT, PASS_BACK = range(9)
LEAD = 4
LAGS = (0, 2, 5, 6, 10)


def kernel(
    amp_hbm, int_hbm, amask_hbm, imask_hbm, out_hbm,
    out, amask, imask, flag_rows, amp, raw, weights, keep, masked, near, mine, other, from_core, part, from_x, total,
    row_in, mask_sem, amp_sem, load_sem, z_send, pass_sem, z_recv, core_send, core_recv, x_send, x_recv,
):
    me = lax.axis_index("wide")
    nar = lax.axis_index("narrow")
    y, z = me // 8, me % 8
    x, core = nar // 2, nar % 2
    turn = 1 - 2 * core
    has_front = (z + turn >= 0) & (z + turn < 8)
    has_back = (z - turn >= 0) & (z - turn < 8)
    front_w, back_w = me + turn, me - turn
    any_front = (front_w >= 0) & (front_w < 64)
    any_back = (back_w >= 0) & (back_w < 64)
    cross_front = any_front & jnp.logical_not(has_front)
    cross_back = any_back & jnp.logical_not(has_back)
    ring_front, ring_back = y * 8 + (z + 8 + turn) % 8, y * 8 + (z + 8 - turn) % 8
    past_y, prior_y = y + turn, y - turn
    pass_past = jnp.logical_not(has_back) & (past_y >= 0) & (past_y < 8)
    pass_prior = jnp.logical_not(has_front) & (prior_y >= 0) & (prior_y < 8)
    partner = {"narrow": x * 2 + 1 - core}

    def greet(device):
        pl.semaphore_signal(pltpu.get_barrier_semaphore(), inc=1, device_id=device, device_id_type=MESH)

    for k in (4, 3, 5, 2, 6, 1, 7):
        greet({"wide": y * 8 + (z + k) % 8})
        greet({"wide": (y + k) % 8 * 8 + z})
    for k in (2, 1, 3):
        greet({"narrow": (x + k) % 4 * 2 + core})
    greet(partner)
    load_amask = pltpu.make_async_copy(amask_hbm, amask, mask_sem.at[0])
    load_imask = pltpu.make_async_copy(imask_hbm, imask, mask_sem.at[1])
    load_amask.start()
    for i in range(8):
        blocks = pl.ds((y + 8 - OFFSETS[i]) % 8 * 8, 8)
        pltpu.make_async_copy(amp_hbm.at[blocks], amp.at[blocks], amp_sem.at[i]).start()
    load_int = pltpu.make_async_copy(int_hbm, raw, load_sem.at[0])
    load_int.start()
    load_imask.start()

    @pl.when(jnp.logical_not(any_front))
    def _():
        near[FRONT] = jnp.zeros((8, 8, 8, 512), jnp.bfloat16)

    @pl.when(jnp.logical_not(any_back))
    def _():
        near[BACK] = jnp.zeros((8, 8, 8, 512), jnp.bfloat16)

    tile = lax.broadcasted_iota(jnp.int32, (512, 512), 1)
    row = lax.broadcasted_iota(jnp.int32, (512, 512), 0)
    load_amask.wait()
    picked = jnp.where(tile // 8 == row // 8, amask[...].astype(jnp.float32), 0.0).astype(jnp.bfloat16)
    spread = jnp.where(row % 8 == tile // TILE, 1.0, 0.0).astype(jnp.bfloat16)
    keep[...] = jnp.dot(picked, spread, preferred_element_type=jnp.float32).astype(jnp.bfloat16).reshape(64, 8, 512)

    def mask_row(i):
        to_y = (y + 8 - OFFSETS[i]) % 8
        blocks = pl.ds(to_y * 8, 8)
        pltpu.make_async_copy(amp_hbm.at[blocks], amp.at[blocks], amp_sem.at[i]).wait()
        masked[blocks] = amp[blocks] * keep[blocks]

    mask_row(0)
    mask_row(1)
    pl.semaphore_wait(pltpu.get_barrier_semaphore(), 18)
    for k in (4, 3, 5, 2, 6, 1, 7):
        pl.semaphore_signal(row_in.at[y], inc=1, device_id={"wide": (y + k) % 8 * 8 + z}, device_id_type=MESH)

    def source(i):
        return (y + OFFSETS[i]) % 8

    def send(i):
        to_y = (y + 8 - OFFSETS[i]) % 8
        if i > 0:
            pl.semaphore_wait(row_in.at[to_y], 1)
        for rel in (4, 3, 5, 2, 6, 1, 7, 0):
            to_z = (z + 8 + turn * rel) % 8
            if rel == 0:
                to, buf, spot, group = to_z, HERE, 0, HERE_SELF
            elif rel <= 4:
                ahead = to_z - turn
                inside = (ahead >= 0) & (ahead < 8)
                to, spot = (ahead + 8) % 8, rel - 1
                buf, group = jnp.where(inside, FRONT, PASS), jnp.where(inside, FRONT_DIRECT, PASS_FRONT)
            else:
                ahead = to_z + turn
                inside = (ahead >= 0) & (ahead < 8)
                to, spot = (ahead + 8) % 8, (rel + 1) % 8
                buf, group = jnp.where(inside, BACK, PASS), jnp.where(inside, BACK_DIRECT, PASS_BACK)
            slab, place, sem = masked.at[to_y * 8 + to_z], near.at[buf, y, spot], z_recv.at[group, y]
            if i == 0 and rel in (0, 1, 7):
                pltpu.make_async_copy(slab, place, sem).start()
            else:
                pltpu.make_async_remote_copy(
                    src_ref=slab, dst_ref=place, send_sem=z_send.at[0], recv_sem=sem,
                    device_id={"wide": to_y * 8 + to}, device_id_type=MESH,
                ).start()

    def arrive(group, c, count):
        span = near.at[HERE, c, pl.ds(0, count)]
        pltpu.make_async_copy(span, span, z_recv.at[group, c]).wait()

    def hand(way, buf, c, first, count, to, to_buf, to_first, group):
        pltpu.make_async_remote_copy(
            src_ref=near.at[buf, c, pl.ds(first, count)], dst_ref=near.at[to_buf, c, pl.ds(to_first, count)],
            send_sem=pass_sem.at[way], recv_sem=z_recv.at[group, c], device_id={"wide": to}, device_id_type=MESH,
        ).start()

    def enter(i):
        c = source(i)
        arrive(jnp.where(has_front, FRONT_DIRECT, PASS_FRONT), c, 4)
        buf = jnp.where(has_front, FRONT, PASS)
        hand(0, buf, c, 0, 4, ring_front, HERE, 1, HERE_FORTH)

        @pl.when(pass_prior)
        def _():
            hand(2, PASS, c, 0, 4, prior_y * 8 + z, FRONT, 0, FRONT_DIRECT)

        arrive(jnp.where(has_back, BACK_DIRECT, PASS_BACK), c, 3)
        buf = jnp.where(has_back, BACK, PASS)
        hand(1, buf, c, 6, 2, ring_back, HERE, 5, HERE_REAR)
        hand(1, buf, c, 0, 1, ring_back, HERE, 7, HERE_REAR)

        @pl.when(pass_past)
        def _():
            hand(2, PASS, c, 6, 2, past_y * 8 + z, BACK, 6, BACK_DIRECT)
            hand(2, PASS, c, 0, 1, past_y * 8 + z, BACK, 0, BACK_DIRECT)

    def relay(i):
        c = source(i)
        arrive(HERE_SELF, c, 1)
        arrive(HERE_FORTH, c, 4)

        @pl.when(any_front)
        def _():
            hand(0, HERE, c, 0, 5, front_w, BACK, 1, BACK_CHAIN)

        arrive(HERE_REAR, c, 3)

        @pl.when(any_back)
        def _():
            hand(1, HERE, c, 5, 3, back_w, FRONT, 4, FRONT_CHAIN)
            hand(1, HERE, c, 0, 1, back_w, FRONT, 7, FRONT_CHAIN)

    def turn_of(i):
        inner, first, last = (OFFSETS[order[i]] for order in TURNS)
        return (y + jnp.where(z == 0, first, jnp.where(z == 7, last, inner))) % 8

    def multiply(i):
        c = turn_of(i)

        @pl.when(any_front)
        def _():
            arrive(FRONT_CHAIN, c, 4)

        @pl.when(cross_front)
        def _():
            arrive(FRONT_DIRECT, c, 4)

        @pl.when(any_back)
        def _():
            arrive(BACK_CHAIN, c, 5)

        @pl.when(cross_back)
        def _():
            arrive(BACK_DIRECT, c, 3)

        acc = None
        for buf in (HERE, FRONT, BACK):
            start = pl.multiple_of((1 + turn * (1 - buf)) * 512, 512)
            term = jnp.dot(
                near[buf, c].reshape(64, 512), weights[pl.ds(start, 512), :], preferred_element_type=jnp.float32
            )
            acc = term if acc is None else acc + term
        mine[i] = acc[:, :256]
        other[i] = acc[:, 256:]
        pltpu.make_async_remote_copy(
            src_ref=other.at[i], dst_ref=from_core.at[i], send_sem=core_send.at[0],
            recv_sem=core_recv.at[i], device_id=partner, device_id_type=MESH,
        ).start()

    low_lanes = lax.broadcasted_iota(jnp.int32, (32, 128), 1) < 64

    def swap(i):
        pltpu.make_async_copy(from_core.at[i], from_core.at[i], core_recv.at[i]).wait()
        for pair in range(2):
            lanes = slice(pair * 128, pair * 128 + 128)
            rows = [
                mine[i, p * 8:p * 8 + 8, lanes] + from_core[i, (8 - p) % 8 * 8:(8 - p) % 8 * 8 + 8, lanes]
                for p in range(8)
            ]
            upper, lower = jnp.concatenate(rows[:4], 0), jnp.concatenate(rows[4:], 0)
            part[i, 2 * pair] = jnp.where(low_lanes, upper, pltpu.roll(lower, 64, 1))
            part[i, 2 * pair + 1] = jnp.where(low_lanes, pltpu.roll(upper, 64, 1), lower)
        for k in (2, 1, 3):
            to = (x + k) % 4
            pltpu.make_async_remote_copy(
                src_ref=part.at[i, to], dst_ref=from_x.at[i, k - 1], send_sem=x_send.at[0],
                recv_sem=x_recv.at[i], device_id={"narrow": to * 2 + core}, device_id_type=MESH,
            ).start()

    def finish(i):
        c = turn_of(i)
        pltpu.make_async_copy(from_x.at[i], from_x.at[i], x_recv.at[i]).wait()
        done = part[i, x] + from_x[i, 0] + from_x[i, 1] + from_x[i, 2]
        turned = pltpu.roll(done, 64, 1)
        for p in range(8):
            at = (z + 8 - turn * p) % 8
            total[c * 8 + at] = (done if p < 4 else turned)[p % 4 * 8:p % 4 * 8 + 8]

    def mask_weights():
        col = lax.broadcasted_iota(jnp.int32, (24, 1536), 1)
        tile = lax.broadcasted_iota(jnp.int32, (24, 1536), 0)
        spread = jnp.where(col // TILE == tile, 1.0, 0.0).astype(jnp.bfloat16)
        load_imask.wait()
        flags = jnp.dot(imask[...].astype(jnp.bfloat16), spread, preferred_element_type=jnp.float32)
        where = lax.broadcasted_iota(jnp.int32, (8, 1536), 1) // 512 + me
        flags = jnp.where((where >= 1) & (where <= 64), flags, 0.0)
        load_int.wait()
        flag_rows[...] = flags
        for half in range(2):
            for pair in range(2):
                parts = []
                for k in range(2):
                    m = 2 * (2 * pair + k) + (core + half) % 2
                    rows = raw[pl.ds(pl.multiple_of(m * 64, 64), 64), :]
                    parts.append(rows * flag_rows[pl.ds(m, 1), :].astype(jnp.bfloat16))
                lanes = slice(half * 256 + pair * 128, half * 256 + pair * 128 + 128)
                weights[:, lanes] = jnp.concatenate(parts, 0).T

    send(0)
    for i in range(2, 8):
        mask_row(i)
    for i in range(1, LEAD):
        send(i)
    stages = (enter, relay, multiply, swap, finish)
    for step in range(8 + LAGS[-1]):
        if step + LEAD < 8:
            send(step + LEAD)
        if step == 2:
            mask_weights()
        for stage, lag in zip(stages, LAGS):
            if 0 <= step - lag < 8:
                stage(step - lag)

    out[...] = total[...].reshape(512, 128).T[:64]
    store = pltpu.make_async_copy(out, out_hbm, mask_sem.at[0])
    store.start()

    def drain(ref, sem):
        pltpu.make_async_copy(ref, ref, sem).wait()

    drain(near.at[0, pl.ds(0, 7)], z_send.at[0])
    drain(near.at[0, 7, pl.ds(0, 5)], z_send.at[0])
    drain(near.at[0, pl.ds(0, 4)], pass_sem.at[0])
    drain(near.at[0, pl.ds(0, 3)], pass_sem.at[1])

    @pl.when(any_front)
    def _():
        drain(near.at[0, pl.ds(0, 5)], pass_sem.at[0])

    @pl.when(any_back)
    def _():
        drain(near.at[0, pl.ds(0, 4)], pass_sem.at[1])

    @pl.when(pass_prior)
    def _():
        drain(near.at[0, pl.ds(0, 4)], pass_sem.at[2])

    @pl.when(pass_past)
    def _():
        drain(near.at[0, pl.ds(0, 3)], pass_sem.at[2])

    drain(other, core_send.at[0])
    drain(from_x, x_send.at[0])
    store.wait()


def body(amplitudes, integrals, amplitude_mask, integral_mask):
    bf16, f32 = jnp.bfloat16, jnp.float32
    dma = pltpu.SemaphoreType.DMA
    return pl.pallas_call(
        kernel,
        out_shape=jax.ShapeDtypeStruct((64, 512), f32),
        in_specs=[
            pl.BlockSpec(memory_space=pl.ANY),
            pl.BlockSpec(memory_space=pl.ANY),
            pl.BlockSpec(memory_space=pl.ANY),
            pl.BlockSpec(memory_space=pl.ANY),
        ],
        out_specs=pl.BlockSpec(memory_space=pl.ANY),
        scratch_shapes=[
            pltpu.VMEM((64, 512), f32),
            pltpu.VMEM((1, 512), jnp.int32),
            pltpu.VMEM((8, 24), jnp.int32),
            pltpu.VMEM((8, 1536), f32),
            pltpu.VMEM((64, 8, 512), bf16),
            pltpu.VMEM((512, 1536), bf16),
            pltpu.VMEM((1536, 512), bf16),
            pltpu.VMEM((64, 8, 512), bf16),
            pltpu.VMEM((64, 8, 512), bf16),
            pltpu.VMEM((4, 8, 8, 8, 512), bf16),
            pltpu.VMEM((8, 64, 256), f32),
            pltpu.VMEM((8, 64, 256), f32),
            pltpu.VMEM((8, 64, 256), f32),
            pltpu.VMEM((8, 4, 32, 128), f32),
            pltpu.VMEM((8, 3, 32, 128), f32),
            pltpu.VMEM((64, 8, 128), f32),
            pltpu.SemaphoreType.REGULAR((8,)),
            dma((2,)),
            dma((8,)),
            dma((1,)),
            dma((1,)),
            dma((3,)),
            dma((9, 8)),
            dma((1,)),
            dma((8,)),
            dma((1,)),
            dma((8,)),
        ],
        compiler_params=pltpu.CompilerParams(
            collective_id=0, has_side_effects=True, vmem_limit_bytes=60 * 1024 * 1024
        ),
        name="ladder",
    )(
        amplitudes.reshape(64, 512, 8).transpose(0, 2, 1),
        integrals[0, 0],
        amplitude_mask.T,
        integral_mask[0, 0],
    )


def solution(mesh):
    return jax.shard_map(
        body,
        mesh=mesh,
        in_specs=(
            P("narrow", "wide"),
            P("narrow", "wide", None, None),
            P("narrow", "wide"),
            P("narrow", "wide", None, None),
        ),
        out_specs=P(("narrow", "wide"), None),
        check_vma=False,
    )
```
